32 devices in a mesh: pb: 4 (over y, x), item: 8 (over z, core).
Axes of the slice: x: 2, y: 2, z: 4, core: 2. Of those that a mesh axis runs over, the one named last changes fastest.
Arguments:
- queries: bfloat16 [2048, 512], P(('pb', 'item')), may hold values from -2 to 2
- gate_query: bfloat16 [2048, 64], P(('pb', 'item')), may hold values from -6 to 250
- items: bfloat16 [4096, 512], P(('item', 'pb')), may hold values from -2 to 2
- gate_items: bfloat16 [4096, 64], P(('item', 'pb')), may hold values from -6 to 6
- slot_tiles: int32 [4, 48], P('pb', 'item'), may hold values from -1 to 15, as said below
- d_scores: bfloat16 [4, 48, 128, 128], P('pb', 'item'), may hold values from -6 to 6
Outputs:
- grad_queries: bfloat16 [2048, 512], P(('pb', 'item'))
- grad_gate_query: float32 [2048, 64], P(('pb', 'item'))
- grad_items: bfloat16 [4096, 512], P(('item', 'pb'))
- grad_gate_items: float32 [4096, 64], P(('item', 'pb'))
The draws below stay inside these ranges and needn't reach their ends.
Inputs may be any that keep to these rules, and one draw needn't show every extreme that they name: `slot_tiles`: each device's row of slots names distinct tiles, live ones first and -1 after them. Devices (p, j) and (p, j + 8 / 2) form a pair: either one of them has all 6 slots live and the other exactly one, or both have between 1 and 3 live slots. Device (0, 0) has all 6 live.
All inputs are finite; a program needn't handle non-finite values.
Results may differ from the reference program's by a relative error of at most 0.0049.
Values may be sent and summed in bfloat16 or wider, within the bound.
A program may use at most 64 MiB of HBM per device.

```python
import jax
import jax.numpy as jnp
from jax import lax

E = 64
KQ = 8
KI = 8
C = 64
TILE = 128
QB_DEV = 4
IT_DEV = 4
SLOTS = 6
NQ = 2048
NI = 4096
N_PB = 4
N_ITEM = 8


def draw_gate_query(key, part):
    subkeys = jax.random.split(key, 1)
    drawn = jnp.clip(1.5 * jax.random.normal(subkeys[0], (NQ, C), jnp.float32), -6.0, 6.0)
    return drawn.astype(jnp.bfloat16)


def draw_slot_tiles(key, part):
    devices_all = N_PB * N_ITEM
    half_item = N_ITEM // 2
    tile_total = QB_DEV * IT_DEV
    light_top = max(SLOTS // 2, 1)
    subkeys = jax.random.split(key, 5)
    pair_kind = jax.random.randint(subkeys[0], (N_PB, half_item), 0, 4)
    pair_kind = pair_kind.at[0, 0].set(0)
    full_side = jax.random.randint(subkeys[1], (N_PB, half_item), 0, 2)
    full_side = full_side.at[0, 0].set(0)
    light_low = jax.random.randint(subkeys[2], (N_PB, half_item), 1, light_top + 1)
    light_high = jax.random.randint(subkeys[3], (N_PB, half_item), 1, light_top + 1)
    skewed = pair_kind == 0
    count_low = jnp.where(skewed, jnp.where(full_side == 0, SLOTS, 1), light_low)
    count_high = jnp.where(skewed, jnp.where(full_side == 1, SLOTS, 1), light_high)
    counts = jnp.concatenate([count_low, count_high], axis=1).reshape(devices_all)
    scores = jax.random.randint(subkeys[4], (devices_all, tile_total), 0, 1048576) * tile_total + jnp.arange(tile_total)[None, :]
    order = jnp.argsort(scores, axis=1, stable=True)[:, :SLOTS]
    places = jnp.arange(SLOTS)[None, :]
    chosen = jnp.where(places < counts[:, None], order, -1)
    return chosen.reshape(N_PB, N_ITEM * SLOTS).astype(jnp.int32)


def levels(rng, shape, cuts, low, high):
    def one(dim, parts):
        heights = jax.random.uniform(jax.random.fold_in(jax.random.fold_in(rng, 6), dim), (parts,), jnp.float32, low / len(cuts), high / len(cuts))
        return jnp.repeat(jnp.exp(heights), shape[dim] // parts).reshape((-1,) + (1,) * (len(shape) - dim - 1))

    level = one(*cuts[0])
    for cut in cuts[1:]:
        level = level * one(*cut)
    return level


def normal_values(key, shape, spread, reach, pieces=(), kind=jnp.bfloat16):
    values = jax.random.normal(key, shape, jnp.float32) * spread
    if len(pieces) > 0:
        values = levels(key, shape, pieces, -0.22, 0.18) * values
    return jnp.clip(values, min=-reach, max=reach).astype(kind)


def setup_inputs(seed: int = 0) -> dict:
    key_of = jax.random.split(jax.random.key(seed), 7)
    return {
        "queries": normal_values(key_of[0], (NQ, KQ * E), 0.35, 2.0, ((0, 32),)),
        "gate_query": draw_gate_query(jax.random.fold_in(key_of[6], 71), 0),
        "items": normal_values(key_of[2], (NI, KI * E), 0.35, 2.0, ((0, 32),)),
        "gate_items": normal_values(key_of[3], (NI, C), 1.5, 6.0, ((0, 32),)),
        "slot_tiles": draw_slot_tiles(jax.random.fold_in(key_of[6], 71), 0),
        "d_scores": normal_values(key_of[5], (N_PB, N_ITEM * SLOTS, TILE, TILE), 1.0, 6.0, ((0, 4), (1, 8))),
    }


def tile_grads(query_tile, query_gate, item_tile, item_gate, cotangent):
    extent = query_tile.shape[0]
    query_parts = query_tile.astype(jnp.float32).reshape(extent, KQ, E)
    item_parts = item_tile.astype(jnp.float32).reshape(extent, KI, E)
    logits = jnp.einsum("qae,ibe->abqi", query_parts, item_parts).reshape(KQ * KI, extent, extent)
    gates = query_gate.astype(jnp.float32).T[:, :, None] + item_gate.astype(jnp.float32).T[:, None, :]
    weights = jax.nn.softmax(gates, axis=0)
    score = jnp.sum(weights * logits, axis=0)
    upstream = cotangent.astype(jnp.float32)[None]
    logit_grad = (upstream * weights).astype(jnp.bfloat16).astype(jnp.float32)
    gate_grad = upstream * weights * (logits - score[None])
    logit_parts = logit_grad.reshape(KQ, KI, extent, extent)
    query_grad = jnp.einsum("abqi,ibe->qae", logit_parts, item_parts).reshape(extent, KQ * E)
    item_grad = jnp.einsum("abqi,qae->ibe", logit_parts, query_parts).reshape(extent, KI * E)
    return query_grad, jnp.sum(gate_grad, axis=2).T, item_grad, jnp.sum(gate_grad, axis=1).T


def reference(queries, gate_query, items, gate_items, slot_tiles, d_scores):
    query_rows = TILE * QB_DEV
    item_rows = TILE * IT_DEV
    flat_ids = slot_tiles.reshape(-1).astype(jnp.int32)
    flat_cot = d_scores.reshape(-1, TILE, TILE)
    flat_index = jnp.arange(flat_ids.shape[0], dtype=jnp.int32)
    totals = (jnp.zeros(queries.shape, jnp.float32), jnp.zeros(gate_query.shape, jnp.float32),
              jnp.zeros(items.shape, jnp.float32), jnp.zeros(gate_items.shape, jnp.float32))

    def visit(carry, inputs):
        tile_id, position, cotangent = inputs
        device = position // SLOTS
        pb_index = device // N_ITEM
        item_index = device % N_ITEM
        safe_id = jnp.maximum(tile_id, 0)
        query_start = (pb_index * query_rows + (safe_id // IT_DEV) * TILE).astype(jnp.int32)
        item_start = (item_index * item_rows + (safe_id % IT_DEV) * TILE).astype(jnp.int32)

        def work(current):
            grads = tile_grads(lax.dynamic_slice_in_dim(queries, query_start, TILE, 0),
                               lax.dynamic_slice_in_dim(gate_query, query_start, TILE, 0),
                               lax.dynamic_slice_in_dim(items, item_start, TILE, 0),
                               lax.dynamic_slice_in_dim(gate_items, item_start, TILE, 0), cotangent)
            starts = (query_start, query_start, item_start, item_start)
            return tuple(lax.dynamic_update_slice_in_dim(total, lax.dynamic_slice_in_dim(total, start, TILE, 0) + update, start, 0)
                         for total, update, start in zip(current, grads, starts))

        return lax.cond(tile_id >= 0, work, lambda current: current, carry), None

    totals, unused = lax.scan(visit, totals, (flat_ids, flat_index, flat_cot))
    return (totals[0].astype(jnp.bfloat16), totals[1], totals[2].astype(jnp.bfloat16), totals[3])
```

```python
import functools

import jax
import jax.numpy as jnp
from jax import lax
from jax.experimental import pallas as pl
from jax.experimental.pallas import tpu as pltpu
from jax.sharding import PartitionSpec as P

E = 64
KQ = 8
KI = 8
C = KQ * KI
MESH = pl.DeviceIdType.MESH
BF = jnp.bfloat16
F32 = jnp.float32
VMEM_BYTES = 48 * 1024 * 1024


def dot_nn(x, y):
    return lax.dot_general(x, y, (((1,), (0,)), ((), ())), preferred_element_type=F32)


def dot_nt(x, y):
    return lax.dot_general(x, y, (((1,), (1,)), ((), ())), preferred_element_type=F32)


def dot_tn(x, y):
    return lax.dot_general(x, y, (((0,), (0,)), ((), ())), preferred_element_type=F32)


def eye(size):
    rows = lax.broadcasted_iota(jnp.int32, (size, size), 0)
    cols = lax.broadcasted_iota(jnp.int32, (size, size), 1)
    return jnp.where(rows == cols, 1.0, 0.0).astype(BF)


def split(x):
    high = x.astype(BF)
    return high, (x - high.astype(F32)).astype(BF)


def greet(devices):
    barrier = pltpu.get_barrier_semaphore()
    for device in devices:
        pl.semaphore_signal(barrier, inc=1, device_id=device, device_id_type=MESH)
    pl.semaphore_wait(barrier, len(devices))


def places(n_pb, n_item):
    p, j = lax.axis_index("pb"), lax.axis_index("item")
    sibling = j + 1 - 2 * lax.rem(j, 2)
    peers = [lax.rem(j + 2 * k, n_item) for k in range(1, n_item // 2)]
    rows = [lax.rem(p + k, n_pb) for k in range(1, n_pb)]
    return p, j, sibling, peers, rows


def send(src, dst, sems, device):
    copy = pltpu.make_async_remote_copy(
        src_ref=src, dst_ref=dst, send_sem=sems[0], recv_sem=sems[1],
        device_id=device, device_id_type=MESH,
    )
    copy.start()
    return copy


def gather_kernel(n_pb, n_item, q_ref, gq_ref, i_ref, gi_ref, bq, bgq, bi, bgi,
                  z_send, z_recv, f_send, f_recv, i_send, i_recv, local_sem):
    p, j, sibling, peers, rows = places(n_pb, n_item)
    greet([(p, sibling)] + [(p, peer) for peer in peers] + [(row, j) for row in rows])
    q_rows, i_rows = q_ref.shape[0], i_ref.shape[0]

    def q_at(ref, index):
        return ref.at[pl.ds(pl.multiple_of(index * q_rows, q_rows), q_rows)]

    def i_at(ref, index):
        return ref.at[pl.ds(pl.multiple_of(index * i_rows, i_rows), i_rows)]

    sides = ((q_ref, bq), (gq_ref, bgq))
    copies, arrivals = [], []
    for k, peer in enumerate(peers):
        arrivals.append([send(src, q_at(dst, j), (z_send.at[k, m], z_recv.at[k, m]), (p, peer))
                         for m, (src, dst) in enumerate(sides)])
    for k, row in enumerate(rows):
        copies += [send(src, i_at(dst, p), (i_send.at[k, m], i_recv.at[k, m]), (row, j))
                   for m, (src, dst) in enumerate(((i_ref, bi), (gi_ref, bgi)))]
    copies += [send(src, q_at(dst, j), (f_send.at[0, m], f_recv.at[0, m]), (p, sibling))
               for m, (src, dst) in enumerate(sides)]
    local = [pltpu.make_async_copy(q_ref, q_at(bq, j), local_sem.at[0]),
             pltpu.make_async_copy(gq_ref, q_at(bgq, j), local_sem.at[1]),
             pltpu.make_async_copy(i_ref, i_at(bi, p), local_sem.at[2]),
             pltpu.make_async_copy(gi_ref, i_at(bgi, p), local_sem.at[3])]
    for copy in local:
        copy.start()
    for k in range(len(peers)):
        source = lax.rem(j + n_item - 2 * (k + 1), n_item)
        for m, dst in enumerate((bq, bgq)):
            arrivals[k][m].wait_recv()
            copies.append(send(q_at(dst, source), q_at(dst, source),
                               (f_send.at[k + 1, m], f_recv.at[k + 1, m]), (p, sibling)))
    for pair in arrivals:
        for copy in pair:
            copy.wait_send()
    for copy in copies:
        copy.wait()
    for copy in local:
        copy.wait()


def gather(n_pb, n_item, queries, gate_query, items, gate_items):
    def whole(x, n):
        return jax.ShapeDtypeStruct((x.shape[0] * n, x.shape[1]), x.dtype)

    half = n_item // 2
    dma = pltpu.SemaphoreType.DMA
    return pl.pallas_call(
        functools.partial(gather_kernel, n_pb, n_item),
        out_shape=(whole(queries, n_item), whole(gate_query, n_item),
                   whole(items, n_pb), whole(gate_items, n_pb)),
        in_specs=[pl.BlockSpec(memory_space=pl.ANY)] * 4,
        out_specs=(pl.BlockSpec(memory_space=pl.ANY),) * 4,
        scratch_shapes=[dma((max(half - 1, 1), 2)), dma((max(half - 1, 1), 2)), dma((half, 2)), dma((half, 2)),
                        dma((max(n_pb - 1, 1), 2)), dma((max(n_pb - 1, 1), 2)), dma((4,))],
        compiler_params=pltpu.CompilerParams(collective_id=0, has_side_effects=True),
        name="gather_blocks",
    )(queries, gate_query, items, gate_items)


def compute_kernel(tiles, bq, bgq, bi, bgi, d_ref, dq, dgq, di, dgi,
                   qt, it, at, bt, qx, ix, s, u, v, dqt, dit, gqt, git):
    nq, width = bq.shape
    ni = bi.shape[0]
    slots, extent = d_ref.shape[0], d_ref.shape[1]
    item_blocks = ni // extent
    eye_w = eye(width)
    eye_c = eye(C)
    qt[...] = dot_nt(eye_w, bq[...])
    it[...] = dot_nt(eye_w, bi[...])

    def gate_factors(ref):
        gates = dot_nt(eye_c, ref[...])
        return jnp.exp(gates - jnp.max(gates, axis=0, keepdims=True))

    at[...] = gate_factors(bgq)
    bt[...] = gate_factors(bgi)
    s[...] = jnp.zeros_like(s)
    dit[...] = jnp.zeros_like(dit)

    def span(a):
        return pl.ds(pl.multiple_of(a * KI * E, KI * E), KI * E)

    @pl.loop(0, KQ)
    def _(a):
        part = qt[pl.ds(pl.multiple_of(a * E, E), E), :]
        a_rows = at[pl.ds(pl.multiple_of(a * KI, KI), KI), :]
        b_rows = bt[pl.ds(pl.multiple_of(a * KI, KI), KI), :]
        for b in range(KI):
            at_b = pl.ds(pl.multiple_of((a * KI + b) * E, E), E)
            qx[at_b, :] = (a_rows[b:b + 1] * part).astype(BF)
            ix[at_b, :] = (b_rows[b:b + 1] * it[b * E:(b + 1) * E, :]).astype(BF)
        s[...] += dot_tn(qx[span(a), :], ix[span(a), :])

    a_high, a_low = split(at[...])
    b_high, b_low = split(bt[...])
    total = dot_tn(jnp.concatenate([a_high, a_high, a_low], axis=0),
                   jnp.concatenate([b_high, b_low, b_high], axis=0))
    for qb in range(nq // extent):
        here = slice(qb * extent, (qb + 1) * extent)
        for ib in range(item_blocks):
            there = slice(ib * extent, (ib + 1) * extent)
            tile_id = qb * item_blocks + ib
            t = jnp.zeros((extent, extent), F32)
            for slot in range(slots):
                t = jnp.where(tiles[0, slot] == tile_id, d_ref[slot].astype(F32), t)
            scale = 1.0 / total[here, there]
            rounded = (t * scale).astype(BF)
            u[here, there] = rounded
            v[here, there] = rounded.astype(F32) * (s[here, there] * scale)

    @pl.loop(0, KQ)
    def _(a):
        item_side = dot_nn(qx[span(a), :], u[...])
        query_side = dot_nt(ix[span(a), :], u[...])
        gates = pl.ds(pl.multiple_of(a * KI, KI), KI)
        a_rows = at[gates, :]
        b_rows = bt[gates, :]
        query_sum = jnp.zeros((E, nq), F32)
        query_rows, item_rows = [], []
        for b in range(KI):
            rows = slice(b * E, (b + 1) * E)
            at_b = pl.ds(pl.multiple_of((a * KI + b) * E, E), E)
            query_sum += a_rows[b:b + 1] * query_side[rows]
            query_rows.append(jnp.sum(qx[at_b, :].astype(F32) * query_side[rows], axis=0, keepdims=True))
            dit[rows, :] += b_rows[b:b + 1] * item_side[rows]
            item_rows.append(jnp.sum(ix[at_b, :].astype(F32) * item_side[rows], axis=0, keepdims=True))
        dqt[pl.ds(pl.multiple_of(a * E, E), E), :] = query_sum.astype(BF)
        gqt[gates, :] = jnp.concatenate(query_rows, axis=0)
        git[gates, :] = jnp.concatenate(item_rows, axis=0)

    v_high, v_low = split(v[...])
    a_both = jnp.concatenate([a_high, a_low], axis=0)
    b_both = jnp.concatenate([b_high, b_low], axis=0)
    q_second = dot_nt(b_both, v_high)
    q_second = q_second[:C] + q_second[C:] + dot_nt(b_high, v_low)
    i_second = dot_nn(a_both, v_high)
    i_second = i_second[:C] + i_second[C:] + dot_nn(a_high, v_low)
    eye_q, eye_i = eye(nq), eye(ni)
    dq[...] = dot_nt(eye_q, dqt[...]).astype(BF)
    di[...] = dot_nt(eye_i, dit[...].astype(BF)).astype(BF)
    dgq[...] = dot_nt(eye_q, (gqt[...] - at[...] * q_second).astype(BF)).astype(BF)
    dgi[...] = dot_nt(eye_i, (git[...] - bt[...] * i_second).astype(BF)).astype(BF)


def compute(slot_tiles, bq, bgq, bi, bgi, d_scores):
    nq, width = bq.shape
    ni = bi.shape[0]
    vmem = pl.BlockSpec(memory_space=pltpu.VMEM)
    scratch = [((width, nq), F32), ((width, ni), F32), ((C, nq), F32), ((C, ni), F32),
               ((C * E, nq), BF), ((C * E, ni), BF), ((nq, ni), F32), ((nq, ni), BF), ((nq, ni), F32),
               ((width, nq), BF), ((width, ni), F32), ((C, nq), F32), ((C, ni), F32)]
    return pl.pallas_call(
        compute_kernel,
        out_shape=tuple(jax.ShapeDtypeStruct(x.shape, BF) for x in (bq, bgq, bi, bgi)),
        in_specs=[pl.BlockSpec(memory_space=pltpu.SMEM)] + [vmem] * 5,
        out_specs=(vmem,) * 4,
        scratch_shapes=[pltpu.VMEM(shape, kind) for shape, kind in scratch],
        compiler_params=pltpu.CompilerParams(vmem_limit_bytes=VMEM_BYTES),
        name="tile_gradients",
    )(slot_tiles, bq, bgq, bi, bgi, d_scores)


def reduce_kernel(n_pb, n_item, dq, dgq, di, dgi, oq, ogq, oi, ogi,
                  near_q, near_g, out_q, out_g, far_q, far_g, item_q, item_g,
                  f_send, f_recv, z_send, z_recv, i_send, i_recv):
    p, j, sibling, peers, rows = places(n_pb, n_item)
    greet([(p, sibling)] + [(p, peer) for peer in peers] + [(row, j) for row in rows])
    q_rows, i_rows = oq.shape[0], oi.shape[0]

    def q_at(index):
        return pl.ds(pl.multiple_of(index * q_rows, q_rows), q_rows)

    def i_at(index):
        return pl.ds(pl.multiple_of(index * i_rows, i_rows), i_rows)

    mine = [j] + peers
    theirs = [x + sibling - j for x in mine]
    order = list(range(1, len(mine))) + [0]
    near = {}
    for k in order:
        near[k] = [send(src.at[q_at(theirs[k])], dst.at[k], (f_send.at[k, m], f_recv.at[k, m]), (p, sibling))
                   for m, (src, dst) in enumerate(((dq, near_q), (dgq, near_g)))]
    item_copies = []
    for k, row in enumerate(rows):
        item_copies += [send(src.at[i_at(row)], dst.at[k], (i_send.at[k, m], i_recv.at[k, m]), (row, j))
                        for m, (src, dst) in enumerate(((di, item_q), (dgi, item_g)))]
    far = []
    for k, peer in enumerate(peers):
        for m, (src, got, staged, dst) in enumerate(((dq, near_q, out_q, far_q), (dgq, near_g, out_g, far_g))):
            near[k + 1][m].wait_recv()
            staged[k] = (src[q_at(peer), :].astype(F32) + got[k + 1].astype(F32)).astype(BF)
            far.append(send(staged.at[k], dst.at[k], (z_send.at[k, m], z_recv.at[k, m]), (p, peer)))
    for copy in near[0]:
        copy.wait_recv()
    for copy in item_copies:
        copy.wait_recv()
    for src, got, out, place in ((di, item_q, oi, i_at(p)), (dgi, item_g, ogi, i_at(p))):
        total = src[place, :].astype(F32)
        for k in range(len(rows)):
            total += got[k].astype(F32)
        out[...] = total.astype(out.dtype)
    for copy in far:
        copy.wait_recv()
    for src, got, more, out in ((dq, near_q, far_q, oq), (dgq, near_g, far_g, ogq)):
        total = src[q_at(j), :].astype(F32) + got[0].astype(F32)
        for k in range(len(peers)):
            total += more[k].astype(F32)
        out[...] = total.astype(out.dtype)
    for k in order:
        for copy in near[k]:
            copy.wait_send()
    for copy in item_copies + far:
        copy.wait_send()


def reduce(n_pb, n_item, dq, dgq, di, dgi):
    half = n_item // 2
    peers, rows = max(half - 1, 1), max(n_pb - 1, 1)
    q_rows, i_rows = dq.shape[0] // n_item, di.shape[0] // n_pb
    width = dq.shape[1]
    dma = pltpu.SemaphoreType.DMA
    vmem = pl.BlockSpec(memory_space=pltpu.VMEM)
    shapes = [(half, q_rows, width), (half, q_rows, C), (peers, q_rows, width), (peers, q_rows, C),
              (peers, q_rows, width), (peers, q_rows, C), (rows, i_rows, width), (rows, i_rows, C)]
    return pl.pallas_call(
        functools.partial(reduce_kernel, n_pb, n_item),
        out_shape=(jax.ShapeDtypeStruct((q_rows, width), BF), jax.ShapeDtypeStruct((q_rows, C), F32),
                   jax.ShapeDtypeStruct((i_rows, width), BF), jax.ShapeDtypeStruct((i_rows, C), F32)),
        in_specs=[vmem] * 4,
        out_specs=(vmem,) * 4,
        scratch_shapes=[pltpu.VMEM(shape, BF) for shape in shapes]
        + [dma((half, 2)), dma((half, 2)), dma((peers, 2)), dma((peers, 2)), dma((rows, 2)), dma((rows, 2))],
        compiler_params=pltpu.CompilerParams(collective_id=1, has_side_effects=True,
                                             vmem_limit_bytes=VMEM_BYTES),
        name="reduce_blocks",
    )(dq, dgq, di, dgi)


def on_device(n_pb, n_item, queries, gate_query, items, gate_items, slot_tiles, d_scores):
    blocks = gather(n_pb, n_item, queries, gate_query, items, gate_items)
    extent = d_scores.shape[-1]
    partial = compute(slot_tiles, *blocks, d_scores.reshape(-1, extent, extent))
    return reduce(n_pb, n_item, *partial)


def solution(mesh):
    return jax.shard_map(
        functools.partial(on_device, mesh.shape["pb"], mesh.shape["item"]),
        mesh=mesh,
        in_specs=(
            P(("pb", "item"), None),
            P(("pb", "item"), None),
            P(("item", "pb"), None),
            P(("item", "pb"), None),
            P("pb", "item"),
            P("pb", "item", None, None),
        ),
        out_specs=(
            P(("pb", "item"), None),
            P(("pb", "item"), None),
            P(("item", "pb"), None),
            P(("item", "pb"), None),
        ),
        check_vma=False,
    )
```

```python
import functools

import jax
import jax.numpy as jnp
from jax import lax
from jax.experimental import pallas as pl
from jax.experimental.pallas import tpu as pltpu
from jax.sharding import PartitionSpec as P

E = 64
KQ = 8
KI = 8
C = KQ * KI
MESH = pl.DeviceIdType.MESH
BF = jnp.bfloat16
F32 = jnp.float32
VMEM_BYTES = 48 * 1024 * 1024


def dot_nn(x, y):
    return lax.dot_general(x, y, (((1,), (0,)), ((), ())), preferred_element_type=F32)


def dot_nt(x, y):
    return lax.dot_general(x, y, (((1,), (1,)), ((), ())), preferred_element_type=F32)


def dot_tn(x, y):
    return lax.dot_general(x, y, (((0,), (0,)), ((), ())), preferred_element_type=F32)


def eye(size):
    rows = lax.broadcasted_iota(jnp.int32, (size, size), 0)
    cols = lax.broadcasted_iota(jnp.int32, (size, size), 1)
    return jnp.where(rows == cols, 1.0, 0.0).astype(BF)


def split(x):
    high = x.astype(BF)
    return high, (x - high.astype(F32)).astype(BF)


def greet(devices):
    barrier = pltpu.get_barrier_semaphore()
    for device in devices:
        pl.semaphore_signal(barrier, inc=1, device_id=device, device_id_type=MESH)
    pl.semaphore_wait(barrier, len(devices))


def places(n_pb, n_item):
    p, j = lax.axis_index("pb"), lax.axis_index("item")
    sibling = j + 1 - 2 * lax.rem(j, 2)
    peers = [lax.rem(j + 2 * k, n_item) for k in range(1, n_item // 2)]
    rows = [lax.rem(p + k, n_pb) for k in range(1, n_pb)]
    return p, j, sibling, peers, rows


def send(src, dst, sems, device):
    copy = pltpu.make_async_remote_copy(
        src_ref=src, dst_ref=dst, send_sem=sems[0], recv_sem=sems[1],
        device_id=device, device_id_type=MESH,
    )
    copy.start()
    return copy


def kernel(n_pb, n_item, tiles, q_ref, gq_ref, i_ref, gi_ref, d_hbm, oq, ogq, oi, ogi,
           bq, bgq, bi, bgi, d_ref, qt, it, at, bt, qx, ix, s, u, v, dqt, dit, gqt, git,
           dq, dgq, di, dgi, near_q, near_g, out_q, out_g, far_q, far_g, item_q, item_g,
           z_send, z_recv, f_send, f_recv, i_send, i_recv,
           rz_send, rz_recv, rf_send, rf_recv, ri_send, ri_recv, local_sem):
    p, j, sibling, peers, others = places(n_pb, n_item)
    greet([(p, sibling)] + [(p, peer) for peer in peers] + [(row, j) for row in others])
    q_rows, i_rows = q_ref.shape[0], i_ref.shape[0]
    nq, width = bq.shape
    ni = bi.shape[0]
    slots, extent = d_ref.shape[0], d_ref.shape[1]
    item_blocks = ni // extent

    def q_at(index):
        return pl.ds(pl.multiple_of(index * q_rows, q_rows), q_rows)

    def i_at(index):
        return pl.ds(pl.multiple_of(index * i_rows, i_rows), i_rows)

    sides = ((q_ref, bq), (gq_ref, bgq))
    copies, arrivals, item_arrivals = [], [], []
    for k, peer in enumerate(peers):
        arrivals.append([send(src, dst.at[q_at(j)], (z_send.at[k, m], z_recv.at[k, m]), (p, peer))
                         for m, (src, dst) in enumerate(sides)])
    for k, row in enumerate(others):
        item_arrivals += [send(i_ref, bi.at[i_at(p)], (i_send.at[k, 0], i_recv.at[k, 0]), (row, j)),
                          send(gi_ref, bgi.at[p], (i_send.at[k, 1], i_recv.at[k, 1]), (row, j))]
    copies += [send(src, dst.at[q_at(j)], (f_send.at[0, m], f_recv.at[0, m]), (p, sibling))
               for m, (src, dst) in enumerate(sides)]
    local = [pltpu.make_async_copy(q_ref, bq.at[q_at(j)], local_sem.at[0]),
             pltpu.make_async_copy(gq_ref, bgq.at[q_at(j)], local_sem.at[1]),
             pltpu.make_async_copy(i_ref, bi.at[i_at(p)], local_sem.at[2]),
             pltpu.make_async_copy(gi_ref, bgi.at[p], local_sem.at[3]),
             pltpu.make_async_copy(d_hbm, d_ref, local_sem.at[4])]
    for copy in local:
        copy.start()
    s[...] = jnp.zeros_like(s)
    dit[...] = jnp.zeros_like(dit)
    for k in range(len(peers)):
        source = lax.rem(j + n_item - 2 * (k + 1), n_item)
        for m, dst in enumerate((bq, bgq)):
            arrivals[k][m].wait_recv()
            copies.append(send(dst.at[q_at(source)], dst.at[q_at(source)],
                               (f_send.at[k + 1, m], f_recv.at[k + 1, m]), (p, sibling)))
    for copy in local:
        copy.wait()
    for copy in item_arrivals:
        copy.wait_recv()

    eye_w = eye(width)

    def factors(gates):
        return jnp.exp(gates - jnp.max(gates, axis=0, keepdims=True))

    it[...] = dot_nt(eye_w, bi[...])
    bt[...] = factors(jnp.concatenate([bgi[k].astype(F32) for k in range(n_pb)], axis=1))
    for copy in copies:
        copy.wait_recv()
    qt[...] = dot_nt(eye_w, bq[...])
    at[...] = factors(dot_nt(eye(C), bgq[...]))

    def span(a):
        return pl.ds(pl.multiple_of(a * KI * E, KI * E), KI * E)

    @pl.loop(0, KQ)
    def _(a):
        part = qt[pl.ds(pl.multiple_of(a * E, E), E), :]
        a_rows = at[pl.ds(pl.multiple_of(a * KI, KI), KI), :]
        b_rows = bt[pl.ds(pl.multiple_of(a * KI, KI), KI), :]
        for b in range(KI):
            at_b = pl.ds(pl.multiple_of((a * KI + b) * E, E), E)
            qx[at_b, :] = (a_rows[b:b + 1] * part).astype(BF)
            ix[at_b, :] = (b_rows[b:b + 1] * it[b * E:(b + 1) * E, :]).astype(BF)
        s[...] += dot_tn(qx[span(a), :], ix[span(a), :])

    a_high, a_low = split(at[...])
    b_high, b_low = split(bt[...])
    total = dot_tn(jnp.concatenate([a_high, a_high, a_low], axis=0),
                   jnp.concatenate([b_high, b_low, b_high], axis=0))
    for qb in range(nq // extent):
        here = slice(qb * extent, (qb + 1) * extent)
        for ib in range(item_blocks):
            there = slice(ib * extent, (ib + 1) * extent)
            tile_id = qb * item_blocks + ib
            t = jnp.zeros((extent, extent), F32)
            for slot in range(slots):
                t = jnp.where(tiles[0, slot] == tile_id, d_ref[slot].astype(F32), t)
            scale = 1.0 / total[here, there]
            rounded = (t * scale).astype(BF)
            u[here, there] = rounded
            v[here, there] = rounded.astype(F32) * (s[here, there] * scale)

    @pl.loop(0, KQ)
    def _(a):
        query_side = dot_nt(ix[span(a), :], u[...])
        gates = pl.ds(pl.multiple_of(a * KI, KI), KI)
        a_rows = at[gates, :]
        query_sum = jnp.zeros((E, nq), F32)
        query_rows = []
        for b in range(KI):
            rows = slice(b * E, (b + 1) * E)
            at_b = pl.ds(pl.multiple_of((a * KI + b) * E, E), E)
            query_sum += a_rows[b:b + 1] * query_side[rows]
            query_rows.append(jnp.sum(qx[at_b, :].astype(F32) * query_side[rows], axis=0, keepdims=True))
        dqt[pl.ds(pl.multiple_of(a * E, E), E), :] = query_sum.astype(BF)
        gqt[gates, :] = jnp.concatenate(query_rows, axis=0)

    v_high, v_low = split(v[...])
    q_second = dot_nt(jnp.concatenate([b_high, b_low], axis=0), v_high)
    q_second = q_second[:C] + q_second[C:] + dot_nt(b_high, v_low)
    eye_q, eye_i = eye(nq), eye(ni)
    dq[...] = dot_nt(eye_q, dqt[...]).astype(BF)
    dgq[...] = dot_nt(eye_q, (gqt[...] - at[...] * q_second).astype(BF)).astype(BF)

    mine = [j] + peers
    theirs = [x + sibling - j for x in mine]
    order = list(range(1, len(mine))) + [0]
    near = {}
    for k in order:
        near[k] = [send(src.at[q_at(theirs[k])], dst.at[k], (rf_send.at[k, m], rf_recv.at[k, m]), (p, sibling))
                   for m, (src, dst) in enumerate(((dq, near_q), (dgq, near_g)))]

    def item_step(a):
        item_side = dot_nn(qx[span(a), :], u[...])
        gates = pl.ds(pl.multiple_of(a * KI, KI), KI)
        b_rows = bt[gates, :]
        item_rows = []
        for b in range(KI):
            rows = slice(b * E, (b + 1) * E)
            at_b = pl.ds(pl.multiple_of((a * KI + b) * E, E), E)
            dit[rows, :] += b_rows[b:b + 1] * item_side[rows]
            item_rows.append(jnp.sum(ix[at_b, :].astype(F32) * item_side[rows], axis=0, keepdims=True))
        git[gates, :] = jnp.concatenate(item_rows, axis=0)

    pl.loop(0, KQ // 4)(item_step)
    far = []
    for k, peer in enumerate(peers):
        for m, (src, got, staged, dst) in enumerate(((dq, near_q, out_q, far_q), (dgq, near_g, out_g, far_g))):
            near[k + 1][m].wait_recv()
            staged[k] = (src[q_at(peer), :].astype(F32) + got[k + 1].astype(F32)).astype(BF)
            far.append(send(staged.at[k], dst.at[k], (rz_send.at[k, m], rz_recv.at[k, m]), (p, peer)))
    pl.loop(KQ // 4, KQ)(item_step)

    di[...] = dot_nt(eye_i, dit[...].astype(BF)).astype(BF)
    item_copies = [send(di.at[i_at(row)], item_q.at[k], (ri_send.at[k, 0], ri_recv.at[k, 0]), (row, j))
                   for k, row in enumerate(others)]
    i_second = dot_nn(jnp.concatenate([a_high, a_low], axis=0), v_high)
    i_second = i_second[:C] + i_second[C:] + dot_nn(a_high, v_low)
    gate_sum = (git[...] - bt[...] * i_second).astype(BF)
    for k in range(n_pb):
        dgi[k] = gate_sum[:, k * i_rows:(k + 1) * i_rows]
    item_copies += [send(dgi.at[row], item_g.at[k], (ri_send.at[k, 1], ri_recv.at[k, 1]), (row, j))
                    for k, row in enumerate(others)]

    for copy in near[0] + far:
        copy.wait_recv()
    for src, got, more, out in ((dq, near_q, far_q, oq), (dgq, near_g, far_g, ogq)):
        total = src[q_at(j), :].astype(F32) + got[0].astype(F32)
        for k in range(len(peers)):
            total += more[k].astype(F32)
        out[...] = total.astype(out.dtype)
    for copy in item_copies:
        copy.wait_recv()
    for own, got, out in ((di[i_at(p), :], item_q, oi), (dgi[p], item_g, ogi)):
        total = own.astype(F32)
        for k in range(len(others)):
            total += got[k].astype(F32)
        out[...] = total.astype(out.dtype)
    for pair in arrivals + [near[k] for k in order]:
        for copy in pair:
            copy.wait_send()
    for copy in copies + item_arrivals + item_copies + far:
        copy.wait_send()


def on_device(n_pb, n_item, queries, gate_query, items, gate_items, slot_tiles, d_scores):
    extent = d_scores.shape[-1]
    cotangents = d_scores.reshape(-1, extent, extent)
    q_rows, width = queries.shape
    i_rows = items.shape[0]
    nq, ni = q_rows * n_item, i_rows * n_pb
    half = n_item // 2
    peers, others = max(half - 1, 1), max(n_pb - 1, 1)
    vmem = pl.BlockSpec(memory_space=pltpu.VMEM)
    hbm = pl.BlockSpec(memory_space=pl.ANY)
    scratch = [((nq, width), BF), ((nq, C), BF), ((ni, width), BF), ((n_pb, C, i_rows), BF), (cotangents.shape, BF),
               ((width, nq), F32), ((width, ni), F32), ((C, nq), F32), ((C, ni), F32),
               ((C * E, nq), BF), ((C * E, ni), BF), ((nq, ni), F32), ((nq, ni), BF), ((nq, ni), F32),
               ((width, nq), BF), ((width, ni), F32), ((C, nq), F32), ((C, ni), F32),
               ((nq, width), BF), ((nq, C), BF), ((ni, width), BF), ((n_pb, C, i_rows), BF),
               ((half, q_rows, width), BF), ((half, q_rows, C), BF), ((peers, q_rows, width), BF), ((peers, q_rows, C), BF),
               ((peers, q_rows, width), BF), ((peers, q_rows, C), BF), ((others, i_rows, width), BF), ((others, C, i_rows), BF)]
    sems = [(peers, 2), (peers, 2), (half, 2), (half, 2), (others, 2), (others, 2)] * 2 + [(5,)]
    out = pl.pallas_call(
        functools.partial(kernel, n_pb, n_item),
        out_shape=(jax.ShapeDtypeStruct((q_rows, width), BF), jax.ShapeDtypeStruct((q_rows, C), F32),
                   jax.ShapeDtypeStruct((i_rows, width), BF), jax.ShapeDtypeStruct((C, i_rows), F32)),
        in_specs=[pl.BlockSpec(memory_space=pltpu.SMEM)] + [hbm] * 5,
        out_specs=(vmem,) * 4,
        scratch_shapes=[pltpu.VMEM(shape, kind) for shape, kind in scratch]
        + [pltpu.SemaphoreType.DMA(shape) for shape in sems],
        compiler_params=pltpu.CompilerParams(collective_id=0, has_side_effects=True, vmem_limit_bytes=VMEM_BYTES),
        name="scoring_backward",
    )(slot_tiles, queries, gate_query, items, gate_items.T, cotangents)
    return out[0], out[1], out[2], out[3].T


def solution(mesh):
    return jax.shard_map(
        functools.partial(on_device, mesh.shape["pb"], mesh.shape["item"]),
        mesh=mesh,
        in_specs=(
            P(("pb", "item"), None),
            P(("pb", "item"), None),
            P(("item", "pb"), None),
            P(("item", "pb"), None),
            P("pb", "item"),
            P("pb", "item", None, None),
        ),
        out_specs=(
            P(("pb", "item"), None),
            P(("pb", "item"), None),
            P(("item", "pb"), None),
            P(("item", "pb"), None),
        ),
        check_vma=False,
    )
```

```python
import functools

import jax
import jax.numpy as jnp
from jax import lax
from jax.experimental import pallas as pl
from jax.experimental.pallas import tpu as pltpu
from jax.sharding import PartitionSpec as P

E = 64
KQ = 8
KI = 8
C = KQ * KI
MESH = pl.DeviceIdType.MESH
BF = jnp.bfloat16
F32 = jnp.float32
VMEM_BYTES = 64 * 1024 * 1024


def dot_nn(x, y):
    return lax.dot_general(x, y, (((1,), (0,)), ((), ())), preferred_element_type=F32)


def dot_nt(x, y):
    return lax.dot_general(x, y, (((1,), (1,)), ((), ())), preferred_element_type=F32)


def dot_tn(x, y):
    return lax.dot_general(x, y, (((0,), (0,)), ((), ())), preferred_element_type=F32)


def eye(size):
    rows = lax.broadcasted_iota(jnp.int32, (size, size), 0)
    cols = lax.broadcasted_iota(jnp.int32, (size, size), 1)
    return jnp.where(rows == cols, 1.0, 0.0).astype(BF)


def split(x):
    high = x.astype(BF)
    return high, (x - high.astype(F32)).astype(BF)


def greet(devices):
    barrier = pltpu.get_barrier_semaphore()
    for device in devices:
        pl.semaphore_signal(barrier, inc=1, device_id=device, device_id_type=MESH)
    pl.semaphore_wait(barrier, len(devices))


def places(n_pb, n_item):
    p, j = lax.axis_index("pb"), lax.axis_index("item")
    sibling = j + 1 - 2 * lax.rem(j, 2)
    peers = [lax.rem(j + 2 * k, n_item) for k in range(1, n_item // 2)]
    half = n_pb // 2
    side, place = p // half, lax.rem(p, half)
    rows = [(1 - side) * half + lax.rem(place + k, half) for k in range(half)]
    rows += [side * half + lax.rem(place + k, half) for k in range(1, half)]
    return p, j, sibling, peers, rows


def send(src, dst, sems, device):
    copy = pltpu.make_async_remote_copy(
        src_ref=src, dst_ref=dst, send_sem=sems[0], recv_sem=sems[1],
        device_id=device, device_id_type=MESH,
    )
    copy.start()
    return copy


def kernel(n_pb, n_item, tiles, q_ref, gq_ref, i_ref, gi_ref, d_hbm, oq, ogq, oi, ogi,
           bq, bgq, bi, bgi, d_ref, qt, it, at, bt, qx, ix, s, u, v, dqt, dit, gqt, git,
           dq, dgq, di, dgi, near_q, near_g, out_q, out_g, far_q, far_g, item_q, item_g,
           z_send, z_recv, f_send, f_recv, i_send, i_recv,
           rz_send, rz_recv, rf_send, rf_recv, ri_send, ri_recv, local_sem):
    p, j, sibling, peers, others = places(n_pb, n_item)
    greet([(p, sibling)] + [(p, peer) for peer in peers] + [(row, j) for row in others])
    q_rows, i_rows = q_ref.shape[0], i_ref.shape[0]
    nq, width = bq.shape
    ni = bi.shape[0]
    slots, extent = d_ref.shape[0], d_ref.shape[1]
    item_blocks = ni // extent

    def q_at(index):
        return pl.ds(pl.multiple_of(index * q_rows, q_rows), q_rows)

    def i_at(index):
        return pl.ds(pl.multiple_of(index * i_rows, i_rows), i_rows)

    sides = ((q_ref, bq), (gq_ref, bgq))
    copies, arrivals, item_arrivals = [], [], []
    for k, peer in enumerate(peers):
        arrivals.append([send(src, dst.at[q_at(j)], (z_send.at[k, m], z_recv.at[k, m]), (p, peer))
                         for m, (src, dst) in enumerate(sides)])
    for k, row in enumerate(others):
        item_arrivals += [send(i_ref, bi.at[i_at(p)], (i_send.at[k, 0], i_recv.at[k, 0]), (row, j)),
                          send(gi_ref, bgi.at[p], (i_send.at[k, 1], i_recv.at[k, 1]), (row, j))]
    copies += [send(src, dst.at[q_at(j)], (f_send.at[0, m], f_recv.at[0, m]), (p, sibling))
               for m, (src, dst) in enumerate(sides)]
    local = [pltpu.make_async_copy(q_ref, bq.at[q_at(j)], local_sem.at[0]),
             pltpu.make_async_copy(gq_ref, bgq.at[q_at(j)], local_sem.at[1]),
             pltpu.make_async_copy(i_ref, bi.at[i_at(p)], local_sem.at[2]),
             pltpu.make_async_copy(gi_ref, bgi.at[p], local_sem.at[3]),
             pltpu.make_async_copy(d_hbm, d_ref, local_sem.at[4])]
    for copy in local:
        copy.start()
    s[...] = jnp.zeros_like(s)
    dit[...] = jnp.zeros_like(dit)
    for k in range(len(peers)):
        source = lax.rem(j + n_item - 2 * (k + 1), n_item)
        for m, dst in enumerate((bq, bgq)):
            arrivals[k][m].wait_recv()
            copies.append(send(dst.at[q_at(source)], dst.at[q_at(source)],
                               (f_send.at[k + 1, m], f_recv.at[k + 1, m]), (p, sibling)))
    for copy in local:
        copy.wait()
    for copy in item_arrivals:
        copy.wait_recv()

    eye_w = eye(width)

    def factors(gates):
        return jnp.exp(gates - jnp.max(gates, axis=0, keepdims=True))

    it[...] = dot_nt(eye_w, bi[...])
    bt[...] = factors(jnp.concatenate([bgi[k].astype(F32) for k in range(n_pb)], axis=1))

    @pl.loop(0, KQ)
    def _(a):
        b_rows = bt[pl.ds(pl.multiple_of(a * KI, KI), KI), :]
        for b in range(KI):
            at_b = pl.ds(pl.multiple_of((a * KI + b) * E, E), E)
            ix[at_b, :] = (b_rows[b:b + 1] * it[b * E:(b + 1) * E, :]).astype(BF)

    for copy in copies:
        copy.wait_recv()
    qt[...] = dot_nt(eye_w, bq[...])
    at[...] = factors(dot_nt(eye(C), bgq[...]))

    def span(a):
        return pl.ds(pl.multiple_of(a * KI * E, KI * E), KI * E)

    @pl.loop(0, KQ)
    def _(a):
        part = qt[pl.ds(pl.multiple_of(a * E, E), E), :]
        a_rows = at[pl.ds(pl.multiple_of(a * KI, KI), KI), :]
        for b in range(KI):
            at_b = pl.ds(pl.multiple_of((a * KI + b) * E, E), E)
            qx[at_b, :] = (a_rows[b:b + 1] * part).astype(BF)
        s[...] += dot_tn(qx[span(a), :], ix[span(a), :])

    a_high, a_low = split(at[...])
    b_high, b_low = split(bt[...])
    total = dot_tn(jnp.concatenate([a_high, a_high, a_low], axis=0),
                   jnp.concatenate([b_high, b_low, b_high], axis=0))
    for qb in range(nq // extent):
        here = slice(qb * extent, (qb + 1) * extent)
        for ib in range(item_blocks):
            there = slice(ib * extent, (ib + 1) * extent)
            tile_id = qb * item_blocks + ib
            t = jnp.zeros((extent, extent), F32)
            for slot in range(slots):
                t = jnp.where(tiles[0, slot] == tile_id, d_ref[slot].astype(F32), t)
            scale = 1.0 / total[here, there]
            rounded = (t * scale).astype(BF)
            u[here, there] = rounded
            v[here, there] = rounded.astype(F32) * (s[here, there] * scale)

    @pl.loop(0, KQ)
    def _(a):
        query_side = dot_nt(ix[span(a), :], u[...])
        gates = pl.ds(pl.multiple_of(a * KI, KI), KI)
        a_rows = at[gates, :]
        query_sum = jnp.zeros((E, nq), F32)
        query_rows = []
        for b in range(KI):
            rows = slice(b * E, (b + 1) * E)
            at_b = pl.ds(pl.multiple_of((a * KI + b) * E, E), E)
            query_sum += a_rows[b:b + 1] * query_side[rows]
            query_rows.append(jnp.sum(qx[at_b, :].astype(F32) * query_side[rows], axis=0, keepdims=True))
        dqt[pl.ds(pl.multiple_of(a * E, E), E), :] = query_sum.astype(BF)
        gqt[gates, :] = jnp.concatenate(query_rows, axis=0)

    v_high, v_low = split(v[...])
    q_second = dot_nt(jnp.concatenate([b_high, b_low], axis=0), v_high)
    q_second = q_second[:C] + q_second[C:] + dot_nt(b_high, v_low)
    eye_q, eye_i = eye(nq), eye(ni // 2)
    dq[...] = dot_nt(eye_q, dqt[...]).astype(BF)
    dgq[...] = dot_nt(eye_q, (gqt[...] - at[...] * q_second).astype(BF)).astype(BF)

    mine = [j] + peers
    theirs = [x + sibling - j for x in mine]
    order = list(range(1, len(mine))) + [0]
    near = {}
    for k in order:
        near[k] = [send(src.at[q_at(theirs[k])], dst.at[k], (rf_send.at[k, m], rf_recv.at[k, m]), (p, sibling))
                   for m, (src, dst) in enumerate(((dq, near_q), (dgq, near_g)))]

    def item_half(part):
        cols = pl.ds(pl.multiple_of(part * (ni // 2), ni // 2), ni // 2)

        @pl.loop(0, KQ)
        def _(a):
            item_side = dot_nn(qx[span(a), :], u[:, cols])
            gates = pl.ds(pl.multiple_of(a * KI, KI), KI)
            b_rows = bt[gates, cols]
            item_rows = []
            for b in range(KI):
                rows = slice(b * E, (b + 1) * E)
                at_b = pl.ds(pl.multiple_of((a * KI + b) * E, E), E)
                dit[rows, cols] += b_rows[b:b + 1] * item_side[rows]
                item_rows.append(jnp.sum(ix[at_b, cols].astype(F32) * item_side[rows], axis=0, keepdims=True))
            git[gates, cols] = jnp.concatenate(item_rows, axis=0)

        di[cols, :] = dot_nt(eye_i, dit[:, cols].astype(BF)).astype(BF)
        high, low = split(v[:, cols])
        second = dot_nn(jnp.concatenate([a_high, a_low], axis=0), high)
        second = second[:C] + second[C:] + dot_nn(a_high, low)
        gate_sum = (git[:, cols] - bt[:, cols] * second).astype(BF)
        for k in range(n_pb // 2):
            dgi[part * (n_pb // 2) + k] = gate_sum[:, k * i_rows:(k + 1) * i_rows]

    def item_sends(first, last):
        sent = []
        for k in range(first, last):
            sent.append(send(di.at[i_at(others[k])], item_q.at[k], (ri_send.at[k, 0], ri_recv.at[k, 0]), (others[k], j)))
            sent.append(send(dgi.at[others[k]], item_g.at[k], (ri_send.at[k, 1], ri_recv.at[k, 1]), (others[k], j)))
        return sent

    side = p // (n_pb // 2)
    item_half(1 - side)
    item_copies = item_sends(0, n_pb // 2)
    far = []
    for k, peer in enumerate(peers):
        for m, (src, got, staged, dst) in enumerate(((dq, near_q, out_q, far_q), (dgq, near_g, out_g, far_g))):
            near[k + 1][m].wait_recv()
            staged[k] = (src[q_at(peer), :].astype(F32) + got[k + 1].astype(F32)).astype(BF)
            far.append(send(staged.at[k], dst.at[k], (rz_send.at[k, m], rz_recv.at[k, m]), (p, peer)))
    item_half(side)
    item_copies += item_sends(n_pb // 2, n_pb - 1)

    for copy in near[0] + far:
        copy.wait_recv()
    for src, got, more, out in ((dq, near_q, far_q, oq), (dgq, near_g, far_g, ogq)):
        total = src[q_at(j), :].astype(F32) + got[0].astype(F32)
        for k in range(len(peers)):
            total += more[k].astype(F32)
        out[...] = total.astype(out.dtype)
    for copy in item_copies:
        copy.wait_recv()
    for own, got, out in ((di[i_at(p), :], item_q, oi), (dgi[p], item_g, ogi)):
        total = own.astype(F32)
        for k in range(len(others)):
            total += got[k].astype(F32)
        out[...] = total.astype(out.dtype)
    for pair in arrivals + [near[k] for k in order]:
        for copy in pair:
            copy.wait_send()
    for copy in copies + item_arrivals + item_copies + far:
        copy.wait_send()


def on_device(n_pb, n_item, queries, gate_query, items, gate_items, slot_tiles, d_scores):
    extent = d_scores.shape[-1]
    cotangents = d_scores.reshape(-1, extent, extent)
    q_rows, width = queries.shape
    i_rows = items.shape[0]
    nq, ni = q_rows * n_item, i_rows * n_pb
    half = n_item // 2
    peers, others = max(half - 1, 1), max(n_pb - 1, 1)
    vmem = pl.BlockSpec(memory_space=pltpu.VMEM)
    hbm = pl.BlockSpec(memory_space=pl.ANY)
    scratch = [((nq, width), BF), ((nq, C), BF), ((ni, width), BF), ((n_pb, C, i_rows), BF), (cotangents.shape, BF),
               ((width, nq), F32), ((width, ni), F32), ((C, nq), F32), ((C, ni), F32),
               ((C * E, nq), BF), ((C * E, ni), BF), ((nq, ni), F32), ((nq, ni), BF), ((nq, ni), F32),
               ((width, nq), BF), ((width, ni), F32), ((C, nq), F32), ((C, ni), F32),
               ((nq, width), BF), ((nq, C), BF), ((ni, width), BF), ((n_pb, C, i_rows), BF),
               ((half, q_rows, width), BF), ((half, q_rows, C), BF), ((peers, q_rows, width), BF), ((peers, q_rows, C), BF),
               ((peers, q_rows, width), BF), ((peers, q_rows, C), BF), ((others, i_rows, width), BF), ((others, C, i_rows), BF)]
    sems = [(peers, 2), (peers, 2), (half, 2), (half, 2), (others, 2), (others, 2)] * 2 + [(5,)]
    out = pl.pallas_call(
        functools.partial(kernel, n_pb, n_item),
        out_shape=(jax.ShapeDtypeStruct((q_rows, width), BF), jax.ShapeDtypeStruct((q_rows, C), F32),
                   jax.ShapeDtypeStruct((i_rows, width), BF), jax.ShapeDtypeStruct((C, i_rows), F32)),
        in_specs=[pl.BlockSpec(memory_space=pltpu.SMEM)] + [hbm] * 5,
        out_specs=(vmem,) * 4,
        scratch_shapes=[pltpu.VMEM(shape, kind) for shape, kind in scratch]
        + [pltpu.SemaphoreType.DMA(shape) for shape in sems],
        compiler_params=pltpu.CompilerParams(collective_id=0, has_side_effects=True, vmem_limit_bytes=VMEM_BYTES),
        name="scoring_backward",
    )(slot_tiles, queries, gate_query, items, gate_items.T, cotangents)
    return out[0], out[1], out[2], out[3].T


def solution(mesh):
    return jax.shard_map(
        functools.partial(on_device, mesh.shape["pb"], mesh.shape["item"]),
        mesh=mesh,
        in_specs=(
            P(("pb", "item"), None),
            P(("pb", "item"), None),
            P(("item", "pb"), None),
            P(("item", "pb"), None),
            P("pb", "item"),
            P("pb", "item", None, None),
        ),
        out_specs=(
            P(("pb", "item"), None),
            P(("pb", "item"), None),
            P(("item", "pb"), None),
            P(("item", "pb"), None),
        ),
        check_vma=False,
    )
```

```python
import functools

import jax
import jax.numpy as jnp
from jax import lax
from jax.experimental import pallas as pl
from jax.experimental.pallas import tpu as pltpu
from jax.sharding import PartitionSpec as P

E = 64
KQ = 8
KI = 8
C = KQ * KI
MESH = pl.DeviceIdType.MESH
BF = jnp.bfloat16
F32 = jnp.float32
VMEM_BYTES = 48 * 1024 * 1024


def dot_nn(x, y):
    return lax.dot_general(x, y, (((1,), (0,)), ((), ())), preferred_element_type=F32)


def dot_nt(x, y):
    return lax.dot_general(x, y, (((1,), (1,)), ((), ())), preferred_element_type=F32)


def dot_tn(x, y):
    return lax.dot_general(x, y, (((0,), (0,)), ((), ())), preferred_element_type=F32)


def eye(size):
    rows = lax.broadcasted_iota(jnp.int32, (size, size), 0)
    cols = lax.broadcasted_iota(jnp.int32, (size, size), 1)
    return jnp.where(rows == cols, 1.0, 0.0).astype(BF)


def split(x):
    high = x.astype(BF)
    return high, (x - high.astype(F32)).astype(BF)


def greet(devices):
    barrier = pltpu.get_barrier_semaphore()
    for device in devices:
        pl.semaphore_signal(barrier, inc=1, device_id=device, device_id_type=MESH)
    pl.semaphore_wait(barrier, len(devices))


def places(n_pb, n_item):
    p, j = lax.axis_index("pb"), lax.axis_index("item")
    sibling = j + 1 - 2 * lax.rem(j, 2)
    peers = [lax.rem(j + 2 * k, n_item) for k in range(1, n_item // 2)]
    half = n_pb // 2
    side, place = p // half, lax.rem(p, half)
    rows = [(1 - side) * half + lax.rem(place + k, half) for k in range(half)]
    rows += [side * half + lax.rem(place + k, half) for k in range(1, half)]
    return p, j, sibling, peers, rows


def send(src, dst, sems, device):
    copy = pltpu.make_async_remote_copy(
        src_ref=src, dst_ref=dst, send_sem=sems[0], recv_sem=sems[1],
        device_id=device, device_id_type=MESH,
    )
    copy.start()
    return copy


def kernel(n_pb, n_item, tiles, q_ref, gq_ref, i_ref, gi_ref, d_hbm, oq, ogq, oi, ogi,
           bq, bgq, bi, bgi, d_ref, qt, it, at, bt, qx, ix, s, u, v, dqt, dit, gqt, git,
           dq, dgq, di, dgi, near_q, near_g, out_q, out_g, far_q, far_g, item_q, item_g,
           z_send, z_recv, f_send, f_recv, i_send, i_recv,
           rz_send, rz_recv, rf_send, rf_recv, ri_send, ri_recv, local_sem):
    p, j, sibling, peers, others = places(n_pb, n_item)
    greet([(p, sibling)] + [(p, peer) for peer in peers] + [(row, j) for row in others])
    q_rows, i_rows = q_ref.shape[0], i_ref.shape[0]
    nq, width = bq.shape
    ni = bi.shape[0]
    slots, extent = d_ref.shape[0], d_ref.shape[1]
    item_blocks = ni // extent

    def q_at(index):
        return pl.ds(pl.multiple_of(index * q_rows, q_rows), q_rows)

    def i_at(index):
        return pl.ds(pl.multiple_of(index * i_rows, i_rows), i_rows)

    sides = ((q_ref, bq), (gq_ref, bgq))
    copies, arrivals, item_arrivals = [], [], []
    for k, peer in enumerate(peers):
        arrivals.append([send(src, dst.at[q_at(j)], (z_send.at[k, m], z_recv.at[k, m]), (p, peer))
                         for m, (src, dst) in enumerate(sides)])
    for k, row in enumerate(others):
        item_arrivals += [send(i_ref, bi.at[i_at(p)], (i_send.at[k, 0], i_recv.at[k, 0]), (row, j)),
                          send(gi_ref, bgi.at[p], (i_send.at[k, 1], i_recv.at[k, 1]), (row, j))]
    copies += [send(src, dst.at[q_at(j)], (f_send.at[0, m], f_recv.at[0, m]), (p, sibling))
               for m, (src, dst) in enumerate(sides)]
    local = [pltpu.make_async_copy(q_ref, bq.at[q_at(j)], local_sem.at[0]),
             pltpu.make_async_copy(gq_ref, bgq.at[q_at(j)], local_sem.at[1]),
             pltpu.make_async_copy(i_ref, bi.at[i_at(p)], local_sem.at[2]),
             pltpu.make_async_copy(gi_ref, bgi.at[p], local_sem.at[3]),
             pltpu.make_async_copy(d_hbm, d_ref, local_sem.at[4])]
    for copy in local:
        copy.start()
    s[...] = jnp.zeros_like(s)
    dit[...] = jnp.zeros_like(dit)
    local[4].wait()
    for qb in range(nq // extent):
        for ib in range(item_blocks):
            tile_id = qb * item_blocks + ib
            t = jnp.zeros((extent, extent), F32)
            for slot in range(slots):
                t = jnp.where(tiles[0, slot] == tile_id, d_ref[slot].astype(F32), t)
            v[qb * extent:(qb + 1) * extent, ib * extent:(ib + 1) * extent] = t
    for k in range(len(peers)):
        source = lax.rem(j + n_item - 2 * (k + 1), n_item)
        for m, dst in enumerate((bq, bgq)):
            arrivals[k][m].wait_recv()
            copies.append(send(dst.at[q_at(source)], dst.at[q_at(source)],
                               (f_send.at[k + 1, m], f_recv.at[k + 1, m]), (p, sibling)))
    for copy in local[:4]:
        copy.wait()
    for copy in item_arrivals:
        copy.wait_recv()

    eye_w = eye(width)

    def factors(gates):
        return jnp.exp(gates - jnp.max(gates, axis=0, keepdims=True))

    it[...] = dot_nt(eye_w, bi[...])
    bt[...] = factors(jnp.concatenate([bgi[k].astype(F32) for k in range(n_pb)], axis=1))

    @pl.loop(0, KQ)
    def _(a):
        b_rows = bt[pl.ds(pl.multiple_of(a * KI, KI), KI), :]
        for b in range(KI):
            at_b = pl.ds(pl.multiple_of((a * KI + b) * E, E), E)
            ix[at_b, :] = (b_rows[b:b + 1] * it[b * E:(b + 1) * E, :]).astype(BF)

    for copy in copies:
        copy.wait_recv()
    qt[...] = dot_nt(eye_w, bq[...])
    at[...] = factors(dot_nt(eye(C), bgq[...]))

    def span(a):
        return pl.ds(pl.multiple_of(a * KI * E, KI * E), KI * E)

    @pl.loop(0, KQ)
    def _(a):
        part = qt[pl.ds(pl.multiple_of(a * E, E), E), :]
        a_rows = at[pl.ds(pl.multiple_of(a * KI, KI), KI), :]
        for b in range(KI):
            at_b = pl.ds(pl.multiple_of((a * KI + b) * E, E), E)
            qx[at_b, :] = (a_rows[b:b + 1] * part).astype(BF)
        s[...] += dot_tn(qx[span(a), :], ix[span(a), :])

    a_high, a_low = split(at[...])
    b_high, b_low = split(bt[...])
    total = dot_tn(jnp.concatenate([a_high, a_high, a_low], axis=0),
                   jnp.concatenate([b_high, b_low, b_high], axis=0))
    for qb in range(nq // extent):
        here = slice(qb * extent, (qb + 1) * extent)
        for ib in range(item_blocks):
            there = slice(ib * extent, (ib + 1) * extent)
            scale = 1.0 / total[here, there]
            rounded = (v[here, there] * scale).astype(BF)
            u[here, there] = rounded
            v[here, there] = rounded.astype(F32) * (s[here, there] * scale)

    @pl.loop(0, KQ)
    def _(a):
        query_side = dot_nt(ix[span(a), :], u[...])
        gates = pl.ds(pl.multiple_of(a * KI, KI), KI)
        a_rows = at[gates, :]
        query_sum = jnp.zeros((E, nq), F32)
        query_rows = []
        for b in range(KI):
            rows = slice(b * E, (b + 1) * E)
            at_b = pl.ds(pl.multiple_of((a * KI + b) * E, E), E)
            query_sum += a_rows[b:b + 1] * query_side[rows]
            query_rows.append(jnp.sum(qx[at_b, :].astype(F32) * query_side[rows], axis=0, keepdims=True))
        dqt[pl.ds(pl.multiple_of(a * E, E), E), :] = query_sum.astype(BF)
        gqt[gates, :] = jnp.concatenate(query_rows, axis=0)

    v_high, v_low = split(v[...])
    q_second = dot_nt(jnp.concatenate([b_high, b_low], axis=0), v_high)
    q_second = q_second[:C] + q_second[C:] + dot_nt(b_high, v_low)
    eye_q, eye_i = eye(nq), eye(ni // 2)
    dq[...] = dot_nt(eye_q, dqt[...]).astype(BF)
    dgq[...] = dot_nt(eye_q, (gqt[...] - at[...] * q_second).astype(BF)).astype(BF)

    mine = [j] + peers
    theirs = [x + sibling - j for x in mine]
    order = list(range(1, len(mine))) + [0]
    near = {}
    for k in order:
        near[k] = [send(src.at[q_at(theirs[k])], dst.at[k], (rf_send.at[k, m], rf_recv.at[k, m]), (p, sibling))
                   for m, (src, dst) in enumerate(((dq, near_q), (dgq, near_g)))]

    def item_half(part):
        cols = pl.ds(pl.multiple_of(part * (ni // 2), ni // 2), ni // 2)

        @pl.loop(0, KQ)
        def _(a):
            item_side = dot_nn(qx[span(a), :], u[:, cols])
            gates = pl.ds(pl.multiple_of(a * KI, KI), KI)
            b_rows = bt[gates, cols]
            item_rows = []
            for b in range(KI):
                rows = slice(b * E, (b + 1) * E)
                at_b = pl.ds(pl.multiple_of((a * KI + b) * E, E), E)
                dit[rows, cols] += b_rows[b:b + 1] * item_side[rows]
                item_rows.append(jnp.sum(ix[at_b, cols].astype(F32) * item_side[rows], axis=0, keepdims=True))
            git[gates, cols] = jnp.concatenate(item_rows, axis=0)

        di[cols, :] = dot_nt(eye_i, dit[:, cols].astype(BF)).astype(BF)
        high, low = split(v[:, cols])
        second = dot_nn(jnp.concatenate([a_high, a_low], axis=0), high)
        second = second[:C] + second[C:] + dot_nn(a_high, low)
        gate_sum = (git[:, cols] - bt[:, cols] * second).astype(BF)
        for k in range(n_pb // 2):
            dgi[part * (n_pb // 2) + k] = gate_sum[:, k * i_rows:(k + 1) * i_rows]

    def item_sends(first, last):
        sent = []
        for k in range(first, last):
            sent.append(send(di.at[i_at(others[k])], item_q.at[k], (ri_send.at[k, 0], ri_recv.at[k, 0]), (others[k], j)))
            sent.append(send(dgi.at[others[k]], item_g.at[k], (ri_send.at[k, 1], ri_recv.at[k, 1]), (others[k], j)))
        return sent

    side = p // (n_pb // 2)
    item_half(1 - side)
    item_copies = item_sends(0, n_pb // 2)
    far = []
    for k, peer in enumerate(peers):
        for m, (src, got, staged, dst) in enumerate(((dq, near_q, out_q, far_q), (dgq, near_g, out_g, far_g))):
            near[k + 1][m].wait_recv()
            staged[k] = (src[q_at(peer), :].astype(F32) + got[k + 1].astype(F32)).astype(BF)
            far.append(send(staged.at[k], dst.at[k], (rz_send.at[k, m], rz_recv.at[k, m]), (p, peer)))
    item_half(side)
    item_copies += item_sends(n_pb // 2, n_pb - 1)

    for copy in near[0] + far:
        copy.wait_recv()
    for src, got, more, out in ((dq, near_q, far_q, oq), (dgq, near_g, far_g, ogq)):
        total = src[q_at(j), :].astype(F32) + got[0].astype(F32)
        for k in range(len(peers)):
            total += more[k].astype(F32)
        out[...] = total.astype(out.dtype)
    for copy in item_copies:
        copy.wait_recv()
    for own, got, out in ((di[i_at(p), :], item_q, oi), (dgi[p], item_g, ogi)):
        total = own.astype(F32)
        for k in range(len(others)):
            total += got[k].astype(F32)
        out[...] = total.astype(out.dtype)
    for pair in arrivals + [near[k] for k in order]:
        for copy in pair:
            copy.wait_send()
    for copy in copies + item_arrivals + item_copies + far:
        copy.wait_send()


def on_device(n_pb, n_item, queries, gate_query, items, gate_items, slot_tiles, d_scores):
    extent = d_scores.shape[-1]
    cotangents = d_scores.reshape(-1, extent, extent)
    q_rows, width = queries.shape
    i_rows = items.shape[0]
    nq, ni = q_rows * n_item, i_rows * n_pb
    half = n_item // 2
    peers, others = max(half - 1, 1), max(n_pb - 1, 1)
    vmem = pl.BlockSpec(memory_space=pltpu.VMEM)
    hbm = pl.BlockSpec(memory_space=pltpu.HBM)
    scratch = [((nq, width), BF), ((nq, C), BF), ((ni, width), BF), ((n_pb, C, i_rows), BF), (cotangents.shape, BF),
               ((width, nq), F32), ((width, ni), F32), ((C, nq), F32), ((C, ni), F32),
               ((C * E, nq), BF), ((C * E, ni), BF), ((nq, ni), F32), ((nq, ni), BF), ((nq, ni), F32),
               ((width, nq), BF), ((width, ni), F32), ((C, nq), F32), ((C, ni), F32),
               ((nq, width), BF), ((nq, C), BF), ((ni, width), BF), ((n_pb, C, i_rows), BF),
               ((half, q_rows, width), BF), ((half, q_rows, C), BF), ((peers, q_rows, width), BF), ((peers, q_rows, C), BF),
               ((peers, q_rows, width), BF), ((peers, q_rows, C), BF), ((others, i_rows, width), BF), ((others, C, i_rows), BF)]
    sems = [(peers, 2), (peers, 2), (half, 2), (half, 2), (others, 2), (others, 2)] * 2 + [(5,)]
    out = pl.pallas_call(
        functools.partial(kernel, n_pb, n_item),
        out_shape=(jax.ShapeDtypeStruct((q_rows, width), BF), jax.ShapeDtypeStruct((q_rows, C), F32),
                   jax.ShapeDtypeStruct((i_rows, width), BF), jax.ShapeDtypeStruct((C, i_rows), F32)),
        in_specs=[pl.BlockSpec(memory_space=pltpu.SMEM)] + [hbm] * 5,
        out_specs=(vmem,) * 4,
        scratch_shapes=[pltpu.VMEM(shape, kind) for shape, kind in scratch]
        + [pltpu.SemaphoreType.DMA(shape) for shape in sems],
        compiler_params=pltpu.CompilerParams(collective_id=0, has_side_effects=True, vmem_limit_bytes=VMEM_BYTES),
        name="scoring_backward",
    )(slot_tiles, *[pltpu.with_memory_space_constraint(x, pltpu.HBM)
                    for x in (queries, gate_query, items, gate_items.T, cotangents)])
    return out[0], out[1], out[2], out[3].T


def solution(mesh):
    return jax.shard_map(
        functools.partial(on_device, mesh.shape["pb"], mesh.shape["item"]),
        mesh=mesh,
        in_specs=(
            P(("pb", "item"), None),
            P(("pb", "item"), None),
            P(("item", "pb"), None),
            P(("item", "pb"), None),
            P("pb", "item"),
            P("pb", "item", None, None),
        ),
        out_specs=(
            P(("pb", "item"), None),
            P(("pb", "item"), None),
            P(("item", "pb"), None),
            P(("item", "pb"), None),
        ),
        check_vma=False,
    )
```
